32 devices in a mesh: wide: 16 (over z, y, core), narrow: 2 (over x).
Axes of the slice: x: 2, y: 2, z: 4, core: 2. Of those that a mesh axis runs over, the one named last changes fastest.
Arguments:
- positions: float32 [3, 512], P(None, ('wide', 'narrow')), may hold values from 0 to 32
- forces: float32 [27, 512], P(None, ('wide', 'narrow')), may hold values from -6 to 6
- owner: int32 [512, 1], P(('wide', 'narrow')), may hold values from 0 to 15; in each aligned block of 16 rows (0 to 15, 16 to 31, ...) at most 2 rows name the same one
Outputs:
- fraction: float32 [3, 1024], P(None, ('wide', 'narrow'))
- velocities: float32 [27, 1024], P(None, ('wide', 'narrow'))
The draws below stay inside these ranges and needn't reach their ends.
Inputs may be any that keep to these rules, and one draw needn't show every extreme that they name: Among the 16 swimmers of one device, at most 2 name the same owner; on some devices some owner is named by exactly 2 of them.
All inputs are finite; a program needn't handle non-finite values.
Results may differ from the reference program's by a relative error of at most 0.0003.
Values sent between devices are 32-bit elements; how exact they have to be, the bound alone decides.
No kernel may reach another device: no remote copies, remote signals or barrier semaphores. Data moves between devices by JAX's collectives and lax.ppermute only.
A program may use at most 64 MiB of HBM per device.

```python
import math
import jax
import jax.numpy as jnp
import numpy as np
from jax import lax

SW_DEV = 16
FIELDS = 9
SWIMMERS = 512
BOX = 32
CAP = 2
N_WIDE = 16
N_NARROW = 2


def shard_levels(key, shape, cuts, smallest, high):
    def one(axis_at, blocks):
        steps = jax.random.uniform(jax.random.fold_in(jax.random.fold_in(key, 6), axis_at), (blocks,), jnp.float32, smallest / len(cuts), high / len(cuts))
        return jnp.repeat(jnp.exp(steps), shape[axis_at] // blocks).reshape((-1,) + (1,) * (len(shape) - axis_at - 1))

    loudness = one(*cuts[0])
    for cut in cuts[1:]:
        loudness = loudness * one(*cut)
    return loudness


def assign_block(rng, own, number, rows, amount, top, bound, slope):
    ranking = jax.random.permutation(rng, amount)
    crowded, usual = load_shares(amount, rows * top, bound, slope, True), load_shares(amount, rows * top, bound, slope, False)
    places = jnp.arange(amount)

    def named(lengths, turn):
        used = int((lengths > 0).sum())
        fixed = max(1, used // 4)
        moved = fixed + (places - fixed + turn * (used - fixed)) % max(1, amount - fixed)
        return jnp.zeros((amount,), jnp.int32).at[ranking[jnp.where(places < fixed, places, moved)]].set(jnp.asarray(lengths, jnp.int32))

    lengths = jnp.where(number % 4 == 0, named(crowded, number // 4), named(usual, number - number // 4 - 1))
    mixed = jax.random.permutation(jax.random.fold_in(own, 3), amount)
    donor, sink = mixed[0:amount // 2 * 2:2], mixed[1:amount // 2 * 2:2]
    slack = jnp.minimum(lengths[donor] - 1, bound - lengths[sink]) // 2
    slack = jnp.where((donor == ranking[0]) | (sink == ranking[0]) | (lengths[sink] == 0), 0, jnp.maximum(slack, 0))
    moved = jax.random.randint(jax.random.fold_in(own, 4), (amount // 2,), 0, 1 << 20) % (slack + 1)
    lengths = lengths.at[donor].add(-moved).at[sink].add(moved)
    labels = jnp.searchsorted(jnp.cumsum(lengths), jnp.arange(rows * top), side="right").astype(jnp.int32)
    listing = labels.reshape(top, rows).T
    listing = listing[jax.random.permutation(jax.random.fold_in(own, 1), rows)]
    turn = jax.random.randint(jax.random.fold_in(own, 2), (rows, 1), 0, top)
    return jnp.take_along_axis(listing, (jnp.arange(top)[None, :] + turn) % top, axis=1)


def load_shares(number_of, total, bound, lean, full):
    portions = [(1 << 20) // math.isqrt(standing ** lean) + 1 for standing in range(1, number_of + 1)]
    largest = bound if full else min(bound, max(-(-total // number_of), total * portions[0] // sum(portions)))
    least = 1 if total - largest >= number_of - 1 else 0
    counts, spare = [largest] + [least] * (number_of - 1), total - largest - least * (number_of - 1)
    while spare > 0:
        movable = [i for i in range(1, number_of) if counts[i] < largest] or [i for i in range(1, number_of) if counts[i] < bound]
        pool, left = sum([portions[i] for i in movable]), spare
        for i in movable:
            extra = min(bound - counts[i], max(1, left * portions[i] // pool), spare)
            counts[i] = counts[i] + extra
            spare = spare - extra
    return np.array(counts)


def bell_draw(stream_key, extent, scale, bound, cuts=(), held_as=jnp.bfloat16):
    entries = scale * jax.random.normal(stream_key, extent, jnp.float32)
    if cuts:
        entries = entries * shard_levels(stream_key, extent, cuts, -0.22, 0.18)
    return jnp.clip(entries, -bound, bound).astype(held_as)


def setup_inputs(seed: int = 0) -> dict:
    key_list = jax.random.split(jax.random.key(seed), 4)
    positions = jnp.clip(32.0 * jax.random.uniform(key_list[0], (3, SWIMMERS), jnp.float32) ** shard_levels(key_list[0], (3, SWIMMERS), ((1, 32),), -0.2, 0.2), 0.0, 32.0)
    forces = bell_draw(key_list[1], (3 * FIELDS, SWIMMERS), 1.0, 6.0, ((1, 32),), jnp.float32)
    owner_keys = jax.random.split(jax.random.fold_in(key_list[2], 1), SWIMMERS // SW_DEV)
    owner_turns = jax.random.permutation(jax.random.fold_in(key_list[2], 3), SWIMMERS // SW_DEV)
    owner = jax.vmap(lambda own, number: assign_block(jax.random.fold_in(key_list[2], 2), own, number, SW_DEV, N_WIDE, 1, CAP, 2))(owner_keys, owner_turns).reshape((SWIMMERS, 1))
    return dict(positions=positions, forces=forces, owner=owner)


step_time = 0.5
brown_weight = 0.3

def pair_velocity(targets, sources, fields):
    width = sources.shape[1]
    delta = targets[:, :, None] - sources[:, None, :]
    radius = jnp.sqrt(delta[0] * delta[0] + delta[1] * delta[1] + delta[2] * delta[2])
    safe = jnp.maximum(radius, 0.5)
    inverse = 1.0 / safe
    far = radius >= 2.0
    along = jnp.where(far, 0.75 * inverse * (1.0 + 2.0 / 3.0 * inverse * inverse), 1.0 - 9.0 / 32.0 * radius)
    across = jnp.where(far, 0.75 * inverse * inverse * inverse * (1.0 - 2.0 * inverse * inverse), 3.0 / 32.0 * inverse)
    split = fields.reshape(3, 9, width)
    tiles = {}
    for first in range(3):
        for second in range(first, 3):
            tiles[first, second] = across * delta[first] * delta[second]
    parts = []
    for first in range(3):
        total = jnp.einsum('ts,ks->kt', along, split[first], precision=lax.Precision.HIGHEST)
        for second in range(3):
            tile = tiles[min(first, second), max(first, second)]
            total = total + jnp.einsum('ts,ks->kt', tile, split[second], precision=lax.Precision.HIGHEST)
        parts.append(total)
    return jnp.concatenate(parts, axis=0)

def reference(positions, forces, owner):
    count = positions.shape[1]
    rows = forces.shape[0]
    target_edge = math.gcd(count, 512)
    source_edge = math.gcd(count, 2048)
    source_pos = jnp.moveaxis(positions.reshape(3, count // source_edge, source_edge), 1, 0)
    source_frc = jnp.moveaxis(forces.reshape(rows, count // source_edge, source_edge), 1, 0)

    def one_block(targets):

        def add_block(total, pieces):
            return (total + pair_velocity(targets, pieces[0], pieces[1]), None)
        start = jnp.zeros((rows, targets.shape[1]), jnp.float32)
        result, unused = lax.scan(add_block, start, (source_pos, source_frc))
        return result
    target_blocks = jnp.moveaxis(positions.reshape(3, count // target_edge, target_edge), 1, 0)
    blocks = lax.map(one_block, target_blocks)
    velocity_full = jnp.moveaxis(blocks, 0, 1).reshape(rows, count)
    split = velocity_full.reshape(3, 9, count)
    drift = step_time * split[:, 0] + brown_weight * lax.optimization_barrier(jnp.sum(split[:, 1:], axis=1))
    moved = (positions + drift) / BOX
    dest = owner[:, 0].astype(jnp.int32)
    grouped = dest.reshape(count // SW_DEV, SW_DEV)
    same = grouped[:, :, None] == grouped[:, None, :]
    local = jnp.arange(SW_DEV, dtype=jnp.int32)
    lower = local[None, :] < local[:, None]
    rank = lax.optimization_barrier(jnp.sum(jnp.where(same & lower[None], 1, 0), axis=2)).astype(jnp.int32).reshape(count)
    device = (jnp.arange(count, dtype=jnp.int32) // SW_DEV).astype(jnp.int32)
    wide_src = device // N_NARROW
    narrow_src = device % N_NARROW
    per_device = N_WIDE * CAP
    column = ((dest * N_NARROW + narrow_src) * per_device + wide_src * CAP + rank).astype(jnp.int32)
    total_slots = count // SW_DEV * per_device
    fraction = jnp.zeros((3, total_slots), jnp.float32).at[:, column].set(moved)
    velocities = jnp.zeros((rows, total_slots), jnp.float32).at[:, column].set(velocity_full)
    return (fraction, velocities)
```

```python
import functools

import jax
import jax.numpy as jnp
from jax import lax
from jax.experimental import pallas as pl
from jax.experimental.pallas import tpu as pltpu
from jax.sharding import PartitionSpec as P

BOX = 32

step_time = 0.5
brown_weight = 0.3

LANES = 128
WIDTH = 32
CAP = 2


def pack_kernel(positions, forces, owner, out):
    swimmers, features = forces.shape
    small = jnp.concatenate(
        [
            positions[...],
            owner[...].astype(jnp.float32),
            jnp.zeros((4, swimmers), jnp.float32),
        ],
        axis=0,
    )
    small = jnp.concatenate([small, jnp.zeros((8, LANES - swimmers), jnp.float32)], axis=1)
    turned = small.T[:swimmers, :4]
    wide = jnp.concatenate(
        [forces[...], turned, jnp.zeros((swimmers, WIDTH - features - 4), jnp.float32)], axis=1
    )
    rows = swimmers * WIDTH // LANES
    packed = jnp.concatenate(
        [wide[g * rows : (g + 1) * rows] for g in range(LANES // WIDTH)], axis=1
    )
    out[...] = jnp.broadcast_to(packed[None], out.shape)


def halves(value):
    high = value.astype(jnp.bfloat16)
    return high, (value - high.astype(jnp.float32)).astype(jnp.bfloat16)


def move_kernel(rows, narrow_count, features, gathered, fraction, velocities):
    groups = LANES // WIDTH
    count = features // 3
    targets = velocities.shape[1]
    chunks = gathered.shape[0] // LANES
    mine_wide = lax.axis_index("wide").astype(jnp.float32)
    mine_narrow = lax.axis_index("narrow")
    shape = (targets, LANES)
    slot = lax.broadcasted_iota(jnp.int32, shape, 0)
    lane = lax.broadcasted_iota(jnp.int32, shape, 1)
    source = (slot // CAP) * narrow_count + mine_narrow
    device = lane // rows
    within = lane % rows

    def turned(chunk):
        return gathered[pl.ds(chunk * LANES, LANES), :].T

    def field(block, group, index):
        at = group * WIDTH + index
        return block[at : at + 1, :]

    def found(chunk, block):
        here = device + chunk * (LANES // rows) == source
        return [
            here & (field(block, g, features + 3) == mine_wide) for g in range(groups)
        ]

    none = 1 << 20

    def search(chunk, carry):
        first, last = carry
        block = turned(chunk)
        for g, hit in enumerate(found(chunk, block)):
            first = jnp.minimum(first, jnp.where(hit, within + g * rows, none))
            last = jnp.maximum(last, jnp.where(hit, within + g * rows, -1))
        return first, last

    def over(body, start):
        return body(0, start) if chunks == 1 else lax.fori_loop(0, chunks, body, start)

    first, last = over(search, (jnp.full(shape, none), jnp.full(shape, -1)))
    first = jnp.min(first, axis=1, keepdims=True)
    last = jnp.max(last, axis=1, keepdims=True)
    parity = lax.broadcasted_iota(jnp.int32, (targets, 1), 0) % CAP
    chosen = jnp.where(parity == 0, first, jnp.where(last > first, last, none))
    valid = (chosen >= 0) & (chosen < none)

    def collect(chunk, carry):
        block = turned(chunk)
        carry = list(carry)
        for g, hit in enumerate(found(chunk, block)):
            one = hit & (within + g * rows == chosen)
            for c in range(3):
                carry[c] = carry[c] + jnp.where(one, field(block, g, features + c), 0.0)
        return tuple(carry)

    centre = over(collect, (jnp.zeros(shape, jnp.float32),) * 3)
    centre = [jnp.sum(part, axis=1, keepdims=True) for part in centre]

    def pairs(chunk, total):
        block = turned(chunk)
        lefts, rights = [], []
        for g in range(groups):
            delta = [centre[c] - field(block, g, features + c) for c in range(3)]
            square = delta[0] * delta[0] + delta[1] * delta[1] + delta[2] * delta[2]
            root = jnp.minimum(lax.rsqrt(square), 1e18)
            radius = square * root
            inverse = jnp.minimum(root, 2.0)
            far = radius >= 2.0
            second = inverse * inverse
            along = jnp.where(
                far, inverse * (0.75 + 0.5 * second), 1.0 - 9.0 / 32.0 * radius
            )
            across = inverse * jnp.where(far, second * (0.75 - 1.5 * second), 3.0 / 32.0)
            scaled = [across * delta[c] for c in range(3)]
            lefts.append(
                jnp.concatenate(
                    [along]
                    + [scaled[a] * delta[b] for a in range(3) for b in range(a, 3)],
                    axis=0,
                )
            )
            rights.append(block[g * WIDTH : (g + 1) * WIDTH, :])
        left = jnp.concatenate(lefts, axis=1)
        right = jnp.concatenate(rights, axis=1)
        left_high, left_low = halves(left)
        right = jnp.concatenate(halves(right), axis=0)

        def dot(part):
            return lax.dot_general(
                part, right, (((1,), (1,)), ((), ())), preferred_element_type=jnp.float32
            )

        return total + (dot(left_high) + dot(left_low))

    total = over(pairs, jnp.zeros((7 * targets, 2 * WIDTH), jnp.float32))
    total = total[:, :WIDTH] + total[:, WIDTH:]
    parts = [total[m * targets : (m + 1) * targets] for m in range(7)]
    tile = {}
    at = 1
    for a in range(3):
        for b in range(a, 3):
            tile[a, b] = tile[b, a] = parts[at]
            at += 1
    outs = []
    for c in range(3):
        value = parts[0][:, c * count : (c + 1) * count]
        for e in range(3):
            value = value + tile[c, e][:, e * count : (e + 1) * count]
        outs.append(value)
    wide = jnp.concatenate(
        outs + centre + [jnp.zeros((targets, LANES - features - 3), jnp.float32)], axis=1
    )
    wide = jnp.where(valid, wide, 0.0).T
    velocity = wide[:features]
    velocities[...] = velocity
    for c in range(3):
        lead = velocity[c * count : c * count + 1]
        rest = jnp.sum(velocity[c * count + 1 : (c + 1) * count], axis=0, keepdims=True)
        drift = step_time * lead + brown_weight * rest
        fraction[c : c + 1, :] = (wide[features + c : features + c + 1] + drift) / BOX


def body(positions, forces, owner):
    swimmers = positions.shape[1]
    features = forces.shape[0]
    wide_count = lax.axis_size("wide")
    narrow_count = lax.axis_size("narrow")
    devices = wide_count * narrow_count
    rows = swimmers * WIDTH // LANES
    vmem = pl.BlockSpec(memory_space=pltpu.VMEM)
    packed = pl.pallas_call(
        pack_kernel,
        out_shape=jax.ShapeDtypeStruct((devices, rows, LANES), jnp.float32),
        in_specs=[vmem] * 3,
        out_specs=vmem,
    )(positions, forces.T, owner.reshape(1, swimmers))
    gathered = lax.all_to_all(packed, ("wide", "narrow"), split_axis=0, concat_axis=0)
    gathered = gathered.reshape(devices * rows, LANES)
    slots = wide_count * CAP
    return pl.pallas_call(
        functools.partial(move_kernel, rows, narrow_count, features),
        out_shape=(
            jax.ShapeDtypeStruct((3, slots), jnp.float32),
            jax.ShapeDtypeStruct((features, slots), jnp.float32),
        ),
        in_specs=[vmem],
        out_specs=(vmem, vmem),
    )(gathered)


def solution(mesh):
    return jax.shard_map(
        body,
        mesh=mesh,
        in_specs=(
            P(None, ("wide", "narrow")),
            P(None, ("wide", "narrow")),
            P(("wide", "narrow"), None),
        ),
        out_specs=(P(None, ("wide", "narrow")), P(None, ("wide", "narrow"))),
        check_vma=False,
    )
```

```python
import functools

import jax
import jax.numpy as jnp
from jax import lax
from jax.experimental import pallas as pl
from jax.experimental.pallas import tpu as pltpu
from jax.sharding import PartitionSpec as P

BOX = 32

step_time = 0.5
brown_weight = 0.3

LANES = 128
WIDTH = 32
CAP = 2


def pack_kernel(positions, forces, owner, out):
    swimmers, features = forces.shape
    small = jnp.concatenate(
        [
            positions[...],
            owner[...].astype(jnp.float32),
            jnp.zeros((4, swimmers), jnp.float32),
        ],
        axis=0,
    )
    small = jnp.concatenate([small, jnp.zeros((8, LANES - swimmers), jnp.float32)], axis=1)
    turned = small.T[:swimmers, :4]
    wide = jnp.concatenate(
        [forces[...], turned, jnp.zeros((swimmers, WIDTH - features - 4), jnp.float32)], axis=1
    )
    rows = swimmers * WIDTH // LANES
    packed = jnp.concatenate(
        [wide[g * rows : (g + 1) * rows] for g in range(LANES // WIDTH)], axis=1
    )
    out[...] = jnp.broadcast_to(packed[None], out.shape)


def halves(value):
    high = value.astype(jnp.bfloat16)
    return high, (value - high.astype(jnp.float32)).astype(jnp.bfloat16)


def move_kernel(rows, narrow_count, features, gathered, fraction, velocities):
    groups = LANES // WIDTH
    count = features // 3
    targets = velocities.shape[1]
    chunks = gathered.shape[0] // LANES
    mine_wide = lax.axis_index("wide").astype(jnp.float32)
    mine_narrow = lax.axis_index("narrow")
    shape = (targets, LANES)
    slot = lax.broadcasted_iota(jnp.int32, shape, 0)
    lane = lax.broadcasted_iota(jnp.int32, shape, 1)
    source = (slot // CAP) * narrow_count + mine_narrow
    device = lane // rows
    within = lane % rows

    def turned(chunk):
        return gathered[pl.ds(chunk * LANES, LANES), :].T

    def field(block, group, index):
        at = group * WIDTH + index
        return block[at : at + 1, :]

    def found(chunk, block):
        here = device + chunk * (LANES // rows) == source
        return [
            here & (field(block, g, features + 3) == mine_wide) for g in range(groups)
        ]

    none = 1 << 20

    def search(chunk, carry):
        first, last = carry
        block = turned(chunk)
        for g, hit in enumerate(found(chunk, block)):
            first = jnp.minimum(first, jnp.where(hit, within + g * rows, none))
            last = jnp.maximum(last, jnp.where(hit, within + g * rows, -1))
        return first, last

    def over(body, start):
        return body(0, start) if chunks == 1 else lax.fori_loop(0, chunks, body, start)

    first, last = over(search, (jnp.full(shape, none), jnp.full(shape, -1)))
    first = jnp.min(first, axis=1, keepdims=True)
    last = jnp.max(last, axis=1, keepdims=True)
    parity = lax.broadcasted_iota(jnp.int32, (targets, 1), 0) % CAP
    chosen = jnp.where(parity == 0, first, jnp.where(last > first, last, none))
    valid = (chosen >= 0) & (chosen < none)

    def collect(chunk, carry):
        block = turned(chunk)
        carry = list(carry)
        for g, hit in enumerate(found(chunk, block)):
            one = hit & (within + g * rows == chosen)
            for c in range(3):
                carry[c] = carry[c] + jnp.where(one, field(block, g, features + c), 0.0)
        return tuple(carry)

    centre = over(collect, (jnp.zeros(shape, jnp.float32),) * 3)
    centre = [jnp.sum(part, axis=1, keepdims=True) for part in centre]

    def pairs(chunk, total):
        block = turned(chunk)
        lefts, rights = [], []
        for g in range(groups):
            delta = [centre[c] - field(block, g, features + c) for c in range(3)]
            square = delta[0] * delta[0] + delta[1] * delta[1] + delta[2] * delta[2]
            root = jnp.minimum(lax.rsqrt(square), 1e18)
            radius = square * root
            inverse = jnp.minimum(root, 2.0)
            far = radius >= 2.0
            second = inverse * inverse
            along = jnp.where(
                far, inverse * (0.75 + 0.5 * second), 1.0 - 9.0 / 32.0 * radius
            )
            across = inverse * jnp.where(far, second * (0.75 - 1.5 * second), 3.0 / 32.0)
            scaled = [across * delta[c] for c in range(3)]
            lefts.append(
                jnp.concatenate(
                    [along]
                    + [scaled[a] * delta[b] for a in range(3) for b in range(a, 3)],
                    axis=0,
                )
            )
            rights.append(block[g * WIDTH : (g + 1) * WIDTH, :])
        left = jnp.concatenate(lefts, axis=1)
        right = jnp.concatenate(rights, axis=1)
        left_high, left_low = halves(left)
        right = jnp.concatenate(halves(right), axis=0)

        def dot(part):
            return lax.dot_general(
                part, right, (((1,), (1,)), ((), ())), preferred_element_type=jnp.float32
            )

        return total + (dot(left_high) + dot(left_low))

    total = over(pairs, jnp.zeros((7 * targets, 2 * WIDTH), jnp.float32))
    total = total[:, :WIDTH] + total[:, WIDTH:]
    parts = [total[m * targets : (m + 1) * targets] for m in range(7)]
    tile = {}
    at = 1
    for a in range(3):
        for b in range(a, 3):
            tile[a, b] = tile[b, a] = parts[at]
            at += 1
    outs = []
    for c in range(3):
        value = parts[0][:, c * count : (c + 1) * count]
        for e in range(3):
            value = value + tile[c, e][:, e * count : (e + 1) * count]
        outs.append(value)
    wide = jnp.concatenate(
        outs + centre + [jnp.zeros((targets, LANES - features - 3), jnp.float32)], axis=1
    )
    wide = jnp.where(valid, wide, 0.0).T
    velocity = wide[:features]
    velocities[...] = velocity
    for c in range(3):
        lead = velocity[c * count : c * count + 1]
        rest = jnp.sum(velocity[c * count + 1 : (c + 1) * count], axis=0, keepdims=True)
        drift = step_time * lead + brown_weight * rest
        fraction[c : c + 1, :] = (wide[features + c : features + c + 1] + drift) / BOX


def body(positions, forces, owner):
    swimmers = positions.shape[1]
    features = forces.shape[0]
    wide_count = lax.axis_size("wide")
    narrow_count = lax.axis_size("narrow")
    devices = wide_count * narrow_count
    rows = swimmers * WIDTH // LANES
    vmem = pl.BlockSpec(memory_space=pltpu.VMEM)
    packed = pl.pallas_call(
        pack_kernel,
        out_shape=jax.ShapeDtypeStruct((devices, rows, LANES), jnp.float32),
        in_specs=[vmem] * 3,
        out_specs=vmem,
        compiler_params=pltpu.CompilerParams(vmem_limit_bytes=4 << 20),
    )(positions, forces.T, owner.reshape(1, swimmers))
    gathered = lax.all_to_all(packed, ("wide", "narrow"), split_axis=0, concat_axis=0)
    gathered = gathered.reshape(devices * rows, LANES)
    slots = wide_count * CAP
    return pl.pallas_call(
        functools.partial(move_kernel, rows, narrow_count, features),
        out_shape=(
            jax.ShapeDtypeStruct((3, slots), jnp.float32),
            jax.ShapeDtypeStruct((features, slots), jnp.float32),
        ),
        in_specs=[vmem],
        out_specs=(vmem, vmem),
        compiler_params=pltpu.CompilerParams(vmem_limit_bytes=16 << 20),
    )(gathered)


def solution(mesh):
    return jax.shard_map(
        body,
        mesh=mesh,
        in_specs=(
            P(None, ("wide", "narrow")),
            P(None, ("wide", "narrow")),
            P(("wide", "narrow"), None),
        ),
        out_specs=(P(None, ("wide", "narrow")), P(None, ("wide", "narrow"))),
        check_vma=False,
    )
```

```python
import functools

import jax
import jax.numpy as jnp
from jax import lax
from jax.experimental import pallas as pl
from jax.experimental.pallas import tpu as pltpu
from jax.sharding import PartitionSpec as P

BOX = 32

step_time = 0.5
brown_weight = 0.3

LANES = 128
WIDTH = 32
CAP = 2


def pack_kernel(small, forces, out):
    swimmers, features = forces.shape
    square = jnp.concatenate([small[...], jnp.zeros((4, swimmers), jnp.float32)], axis=0)
    square = jnp.concatenate([square, jnp.zeros((8, LANES - swimmers), jnp.float32)], axis=1)
    turned = square.T[:swimmers, :4]
    wide = jnp.concatenate(
        [forces[...], turned, jnp.zeros((swimmers, WIDTH - features - 4), jnp.float32)], axis=1
    )
    rows = swimmers * WIDTH // LANES
    packed = jnp.concatenate(
        [wide[g * rows : (g + 1) * rows] for g in range(LANES // WIDTH)], axis=1
    )
    out[...] = jnp.broadcast_to(packed[None], out.shape)


def halves(value):
    high = value.astype(jnp.bfloat16)
    return high, (value - high.astype(jnp.float32)).astype(jnp.bfloat16)


def move_kernel(rows, narrow_count, features, gathered, fraction, velocities):
    groups = LANES // WIDTH
    count = features // 3
    targets = velocities.shape[1]
    chunks = gathered.shape[0] // LANES
    mine_wide = lax.axis_index("wide").astype(jnp.float32)
    mine_narrow = lax.axis_index("narrow")
    shape = (targets, LANES)
    slot = lax.broadcasted_iota(jnp.int32, shape, 0)
    lane = lax.broadcasted_iota(jnp.int32, shape, 1)
    source = gathered.shape[0] // rows - 1 - (slot // CAP) * narrow_count - mine_narrow
    device = lane // rows
    within = lane % rows

    def turned(chunk):
        return gathered[pl.ds(chunk * LANES, LANES), :].T

    def field(block, group, index):
        at = group * WIDTH + index
        return block[at : at + 1, :]

    def found(chunk, block):
        here = device + chunk * (LANES // rows) == source
        return [
            here & (field(block, g, features + 3) == mine_wide) for g in range(groups)
        ]

    none = 1 << 20

    def search(chunk, carry):
        first, last = carry
        block = turned(chunk)
        for g, hit in enumerate(found(chunk, block)):
            first = jnp.minimum(first, jnp.where(hit, within + g * rows, none))
            last = jnp.maximum(last, jnp.where(hit, within + g * rows, -1))
        return first, last

    def over(body, start):
        return body(0, start) if chunks == 1 else lax.fori_loop(0, chunks, body, start)

    first, last = over(search, (jnp.full(shape, none), jnp.full(shape, -1)))
    first = jnp.min(first, axis=1, keepdims=True)
    last = jnp.max(last, axis=1, keepdims=True)
    parity = lax.broadcasted_iota(jnp.int32, (targets, 1), 0) % CAP
    chosen = jnp.where(parity == 0, first, jnp.where(last > first, last, none))
    valid = (chosen >= 0) & (chosen < none)

    def collect(chunk, carry):
        block = turned(chunk)
        carry = list(carry)
        for g, hit in enumerate(found(chunk, block)):
            one = hit & (within + g * rows == chosen)
            for c in range(3):
                carry[c] = carry[c] + jnp.where(one, field(block, g, features + c), 0.0)
        return tuple(carry)

    centre = over(collect, (jnp.zeros(shape, jnp.float32),) * 3)
    centre = [jnp.sum(part, axis=1, keepdims=True) for part in centre]

    def pairs(chunk, total):
        block = turned(chunk)
        lefts, rights = [], []
        for g in range(groups):
            delta = [centre[c] - field(block, g, features + c) for c in range(3)]
            square = delta[0] * delta[0] + delta[1] * delta[1] + delta[2] * delta[2]
            root = jnp.minimum(lax.rsqrt(square), 1e18)
            radius = square * root
            inverse = jnp.minimum(root, 2.0)
            far = radius >= 2.0
            second = inverse * inverse
            along = jnp.where(
                far, inverse * (0.75 + 0.5 * second), 1.0 - 9.0 / 32.0 * radius
            )
            across = inverse * jnp.where(far, second * (0.75 - 1.5 * second), 3.0 / 32.0)
            scaled = [across * delta[c] for c in range(3)]
            lefts.append(
                jnp.concatenate(
                    [along]
                    + [scaled[a] * delta[b] for a in range(3) for b in range(a, 3)],
                    axis=0,
                )
            )
            rights.append(block[g * WIDTH : (g + 1) * WIDTH, :])
        left = jnp.concatenate(lefts, axis=1)
        right = jnp.concatenate(rights, axis=1)
        left_high, left_low = halves(left)
        right = jnp.concatenate(halves(right), axis=0)

        def dot(part):
            return lax.dot_general(
                part, right, (((1,), (1,)), ((), ())), preferred_element_type=jnp.float32
            )

        return total + (dot(left_high) + dot(left_low))

    total = over(pairs, jnp.zeros((7 * targets, 2 * WIDTH), jnp.float32))
    total = total[:, :WIDTH] + total[:, WIDTH:]
    parts = [total[m * targets : (m + 1) * targets] for m in range(7)]
    tile = {}
    at = 1
    for a in range(3):
        for b in range(a, 3):
            tile[a, b] = tile[b, a] = parts[at]
            at += 1
    outs = []
    for c in range(3):
        value = parts[0][:, c * count : (c + 1) * count]
        for e in range(3):
            value = value + tile[c, e][:, e * count : (e + 1) * count]
        outs.append(value)
    wide = jnp.concatenate(
        outs + centre + [jnp.zeros((targets, LANES - features - 3), jnp.float32)], axis=1
    )
    wide = jnp.where(valid, wide, 0.0).T
    velocity = wide[:features]
    velocities[...] = velocity
    for c in range(3):
        lead = velocity[c * count : c * count + 1]
        rest = jnp.sum(velocity[c * count + 1 : (c + 1) * count], axis=0, keepdims=True)
        drift = step_time * lead + brown_weight * rest
        fraction[c : c + 1, :] = (wide[features + c : features + c + 1] + drift) / BOX


def body(positions, forces, owner):
    swimmers = positions.shape[1]
    features = forces.shape[0]
    wide_count = lax.axis_size("wide")
    narrow_count = lax.axis_size("narrow")
    devices = wide_count * narrow_count
    rows = swimmers * WIDTH // LANES
    vmem = pl.BlockSpec(memory_space=pltpu.VMEM)
    small = jnp.concatenate([positions.T, owner.astype(jnp.float32)], axis=1).T
    packed = pl.pallas_call(
        pack_kernel,
        out_shape=jax.ShapeDtypeStruct((devices, rows, LANES), jnp.float32),
        in_specs=[vmem] * 2,
        out_specs=vmem,
        compiler_params=pltpu.CompilerParams(vmem_limit_bytes=4 << 20),
    )(small, forces.T)
    order = list(range(devices))[::-1]
    gathered = lax.all_to_all(
        packed, ("wide", "narrow"), split_axis=0, concat_axis=0, axis_index_groups=[order]
    )
    gathered = gathered.reshape(devices * rows, LANES)
    slots = wide_count * CAP
    return pl.pallas_call(
        functools.partial(move_kernel, rows, narrow_count, features),
        out_shape=(
            jax.ShapeDtypeStruct((3, slots), jnp.float32),
            jax.ShapeDtypeStruct((features, slots), jnp.float32),
        ),
        in_specs=[vmem],
        out_specs=(vmem, vmem),
        compiler_params=pltpu.CompilerParams(vmem_limit_bytes=16 << 20),
    )(gathered)


def solution(mesh):
    return jax.shard_map(
        body,
        mesh=mesh,
        in_specs=(
            P(None, ("wide", "narrow")),
            P(None, ("wide", "narrow")),
            P(("wide", "narrow"), None),
        ),
        out_specs=(P(None, ("wide", "narrow")), P(None, ("wide", "narrow"))),
        check_vma=False,
    )
```

```python
import functools

import jax
import jax.numpy as jnp
from jax import lax
from jax.experimental import pallas as pl
from jax.experimental.pallas import tpu as pltpu
from jax.sharding import PartitionSpec as P

BOX = 32

step_time = 0.5
brown_weight = 0.3

LANES = 128
WIDTH = 32
CAP = 2


def pack_kernel(small, forces, out):
    swimmers, features = forces.shape
    rows = swimmers * WIDTH // LANES
    square = jnp.concatenate(
        [
            jnp.zeros((features, swimmers), jnp.float32),
            small[...],
            jnp.zeros((WIDTH - features - 4, swimmers), jnp.float32),
        ],
        axis=0,
    )
    square = jnp.concatenate(
        [square, jnp.full((WIDTH, LANES - swimmers), -1.0, jnp.float32)], axis=1
    )
    row = square[features + 3 : features + 4, :]
    before = pltpu.roll(jnp.broadcast_to(row, (swimmers, LANES)), 1, 1, stride=1, stride_axis=0)
    earlier = lax.broadcasted_iota(jnp.int32, before.shape, 0) < lax.broadcasted_iota(
        jnp.int32, before.shape, 1
    )
    rank = jnp.sum(jnp.where((before == row) & earlier, 1.0, 0.0), axis=0, keepdims=True)
    at = lax.broadcasted_iota(jnp.int32, square.shape, 0)
    square = jnp.where(at == features + 4, rank, square)
    turned = jnp.concatenate(
        [square.T[:swimmers], jnp.zeros((swimmers, LANES - WIDTH), jnp.float32)], axis=1
    )
    first = jnp.concatenate(
        [forces[...], jnp.zeros((swimmers, LANES - features), jnp.float32)], axis=1
    )
    lane = lax.broadcasted_iota(jnp.int32, first.shape, 1)
    wide = jnp.where(lane < features, first, turned)
    packed = wide[:rows]
    for g in range(1, LANES // WIDTH):
        packed = packed + pltpu.roll(wide, g * WIDTH, 1)[g * rows : (g + 1) * rows]
    out[...] = jnp.broadcast_to(packed[None], out.shape)


def halves(value):
    high = value.astype(jnp.bfloat16)
    return high, (value - high.astype(jnp.float32)).astype(jnp.bfloat16)


def move_kernel(rows, narrow_count, features, gathered, fraction, velocities):
    groups = LANES // WIDTH
    count = features // 3
    targets = velocities.shape[1]
    chunks = gathered.shape[0] // LANES
    mine_wide = lax.axis_index("wide").astype(jnp.float32)
    mine_narrow = lax.axis_index("narrow")
    shape = (targets, LANES)
    slot = lax.broadcasted_iota(jnp.int32, shape, 0)
    lane = lax.broadcasted_iota(jnp.int32, shape, 1)
    source = gathered.shape[0] // rows - 1 - (slot // CAP) * narrow_count - mine_narrow
    device = lane // rows
    rank = (slot % CAP).astype(jnp.float32)

    def turned(chunk):
        return gathered[pl.ds(chunk * LANES, LANES), :].T

    def field(block, group, index):
        at = group * WIDTH + index
        return block[at : at + 1, :]

    def over(body, start):
        return body(0, start) if chunks == 1 else lax.fori_loop(0, chunks, body, start)

    def collect(chunk, carry):
        block = turned(chunk)
        here = device + chunk * (LANES // rows) == source
        carry = list(carry)
        for g in range(groups):
            hit = (
                here
                & (field(block, g, features + 3) == mine_wide)
                & (field(block, g, features + 4) == rank)
            )
            for c in range(3):
                carry[c] = carry[c] + jnp.where(hit, field(block, g, features + c), 0.0)
            carry[3] = carry[3] + jnp.where(hit, 1.0, 0.0)
        return tuple(carry)

    centre = over(collect, (jnp.zeros(shape, jnp.float32),) * 4)
    centre = [jnp.sum(part, axis=1, keepdims=True) for part in centre]
    valid = centre.pop() > 0.0

    def pairs(chunk, total):
        block = turned(chunk)
        lefts, rights = [], []
        for g in range(groups):
            delta = [centre[c] - field(block, g, features + c) for c in range(3)]
            square = delta[0] * delta[0] + delta[1] * delta[1] + delta[2] * delta[2]
            root = jnp.minimum(lax.rsqrt(square), 1e18)
            radius = square * root
            inverse = jnp.minimum(root, 2.0)
            far = radius >= 2.0
            second = inverse * inverse
            along = jnp.where(
                far, inverse * (0.75 + 0.5 * second), 1.0 - 9.0 / 32.0 * radius
            )
            across = inverse * jnp.where(far, second * (0.75 - 1.5 * second), 3.0 / 32.0)
            scaled = [across * delta[c] for c in range(3)]
            tiles = [scaled[a] * delta[b] for a in range(3) for b in range(a, 3)]
            lefts.append(
                jnp.concatenate(
                    [along + tile if k in (0, 3, 5) else tile for k, tile in enumerate(tiles)],
                    axis=0,
                )
            )
            rights.append(block[g * WIDTH : (g + 1) * WIDTH, :])
        left = jnp.concatenate(lefts, axis=1)
        right = jnp.concatenate(rights, axis=1)
        left_high, left_low = halves(left)
        right = jnp.concatenate(halves(right), axis=0)

        def dot(part):
            return lax.dot_general(
                right, part, (((1,), (1,)), ((), ())), preferred_element_type=jnp.float32
            )

        return total + (dot(left_high) + dot(left_low))

    total = over(pairs, jnp.zeros((2 * WIDTH, 6 * targets), jnp.float32))
    total = total[:WIDTH] + total[WIDTH:]
    parts = [total[:, m * targets : (m + 1) * targets] for m in range(6)]
    tile = {}
    at = 0
    for a in range(3):
        for b in range(a, 3):
            tile[a, b] = tile[b, a] = parts[at]
            at += 1
    outs = []
    for c in range(3):
        outs.append(sum(tile[c, e][e * count : (e + 1) * count] for e in range(3)))
    rows_of = jnp.concatenate(
        centre + [jnp.where(valid, 1.0, 0.0), jnp.zeros((targets, LANES - 4), jnp.float32)], axis=1
    ).T[:8, :targets]
    there = rows_of[3:4] > 0.0
    wide = jnp.where(there, jnp.concatenate(outs + [rows_of[:3]], axis=0), 0.0)
    velocity = wide[:features]
    velocities[...] = velocity
    for c in range(3):
        lead = velocity[c * count : c * count + 1]
        rest = jnp.sum(velocity[c * count + 1 : (c + 1) * count], axis=0, keepdims=True)
        drift = step_time * lead + brown_weight * rest
        fraction[c : c + 1, :] = (wide[features + c : features + c + 1] + drift) / BOX


def body(positions, forces, owner):
    swimmers = positions.shape[1]
    features = forces.shape[0]
    wide_count = lax.axis_size("wide")
    narrow_count = lax.axis_size("narrow")
    devices = wide_count * narrow_count
    rows = swimmers * WIDTH // LANES
    vmem = pl.BlockSpec(memory_space=pltpu.VMEM)
    small = jnp.concatenate([positions.T, owner.astype(jnp.float32)], axis=1).T
    packed = pl.pallas_call(
        pack_kernel,
        out_shape=jax.ShapeDtypeStruct((devices, rows, LANES), jnp.float32),
        in_specs=[vmem] * 2,
        out_specs=vmem,
        compiler_params=pltpu.CompilerParams(vmem_limit_bytes=4 << 20),
    )(small, forces.T)
    order = list(range(devices))[::-1]
    gathered = lax.all_to_all(
        packed, ("wide", "narrow"), split_axis=0, concat_axis=0, axis_index_groups=[order]
    )
    gathered = gathered.reshape(devices * rows, LANES)
    slots = wide_count * CAP
    return pl.pallas_call(
        functools.partial(move_kernel, rows, narrow_count, features),
        out_shape=(
            jax.ShapeDtypeStruct((3, slots), jnp.float32),
            jax.ShapeDtypeStruct((features, slots), jnp.float32),
        ),
        in_specs=[vmem],
        out_specs=(vmem, vmem),
        compiler_params=pltpu.CompilerParams(vmem_limit_bytes=16 << 20),
    )(gathered)


def solution(mesh):
    return jax.shard_map(
        body,
        mesh=mesh,
        in_specs=(
            P(None, ("wide", "narrow")),
            P(None, ("wide", "narrow")),
            P(("wide", "narrow"), None),
        ),
        out_specs=(P(None, ("wide", "narrow")), P(None, ("wide", "narrow"))),
        check_vma=False,
    )
```

```python
import functools

import jax
import jax.numpy as jnp
from jax import lax
from jax.experimental import pallas as pl
from jax.experimental.pallas import tpu as pltpu
from jax.sharding import PartitionSpec as P

BOX = 32

step_time = 0.5
brown_weight = 0.3

LANES = 128
WIDTH = 32
CAP = 2


def pack_kernel(small, forces, out):
    swimmers, features = forces.shape
    rows = swimmers * WIDTH // LANES
    square = jnp.concatenate(
        [
            jnp.zeros((features, swimmers), jnp.float32),
            small[...],
            jnp.zeros((WIDTH - features - 4, swimmers), jnp.float32),
        ],
        axis=0,
    )
    square = jnp.concatenate(
        [square, jnp.full((WIDTH, LANES - swimmers), -1.0, jnp.float32)], axis=1
    )
    row = square[features + 3 : features + 4, :]
    before = pltpu.roll(jnp.broadcast_to(row, (swimmers, LANES)), 1, 1, stride=1, stride_axis=0)
    earlier = lax.broadcasted_iota(jnp.int32, before.shape, 0) < lax.broadcasted_iota(
        jnp.int32, before.shape, 1
    )
    rank = jnp.sum(jnp.where((before == row) & earlier, 1.0, 0.0), axis=0, keepdims=True)
    at = lax.broadcasted_iota(jnp.int32, square.shape, 0)
    square = jnp.where(at == features + 4, rank, square)
    turned = jnp.concatenate(
        [square.T[:swimmers], jnp.zeros((swimmers, LANES - WIDTH), jnp.float32)], axis=1
    )
    first = jnp.concatenate(
        [forces[...], jnp.zeros((swimmers, LANES - features), jnp.float32)], axis=1
    )
    lane = lax.broadcasted_iota(jnp.int32, first.shape, 1)
    wide = jnp.where(lane < features, first, turned)
    packed = wide[:rows]
    for g in range(1, LANES // WIDTH):
        packed = packed + pltpu.roll(wide, g * WIDTH, 1)[g * rows : (g + 1) * rows]
    out[...] = jnp.broadcast_to(packed[None], out.shape)


def halves(value):
    high = value.astype(jnp.bfloat16)
    return high, (value - high.astype(jnp.float32)).astype(jnp.bfloat16)


def move_kernel(rows, narrow_count, features, own, other, fraction, velocities):
    groups = LANES // WIDTH
    count = features // 3
    targets = velocities.shape[1]
    half = LANES // 2
    chunks = own.shape[0] // half
    side = own.shape[0] // rows
    index = lax.axis_index("wide")
    mine_wide = index.astype(jnp.float32)
    mine_narrow = lax.axis_index("narrow")
    shape = (targets, LANES)
    slot = lax.broadcasted_iota(jnp.int32, shape, 0)
    lane = lax.broadcasted_iota(jnp.int32, shape, 1)
    giver = slot // CAP
    source = side - 1 - giver // 2 * narrow_count - mine_narrow
    source = source + jnp.where(giver % 2 == index % 2, 0, side)
    device = lane // half * side + lane % half // rows
    rank = (slot % CAP).astype(jnp.float32)

    def turned(chunk):
        at = pl.ds(chunk * half, half)
        return jnp.concatenate([own[at, :], other[at, :]], axis=0).T

    def field(block, group, index):
        at = group * WIDTH + index
        return block[at : at + 1, :]

    def over(body, start):
        return body(0, start) if chunks == 1 else lax.fori_loop(0, chunks, body, start)

    def collect(chunk, carry):
        block = turned(chunk)
        here = device + chunk * (half // rows) == source
        carry = list(carry)
        for g in range(groups):
            hit = (
                here
                & (field(block, g, features + 3) == mine_wide)
                & (field(block, g, features + 4) == rank)
            )
            for c in range(3):
                carry[c] = carry[c] + jnp.where(hit, field(block, g, features + c), 0.0)
            carry[3] = carry[3] + jnp.where(hit, 1.0, 0.0)
        return tuple(carry)

    centre = over(collect, (jnp.zeros(shape, jnp.float32),) * 4)
    centre = [jnp.sum(part, axis=1, keepdims=True) for part in centre]
    valid = centre.pop() > 0.0

    def pairs(chunk, total):
        block = turned(chunk)
        lefts, rights = [], []
        for g in range(groups):
            delta = [centre[c] - field(block, g, features + c) for c in range(3)]
            square = delta[0] * delta[0] + delta[1] * delta[1] + delta[2] * delta[2]
            root = jnp.minimum(lax.rsqrt(square), 1e18)
            radius = square * root
            inverse = jnp.minimum(root, 2.0)
            far = radius >= 2.0
            second = inverse * inverse
            along = jnp.where(
                far, inverse * (0.75 + 0.5 * second), 1.0 - 9.0 / 32.0 * radius
            )
            across = inverse * jnp.where(far, second * (0.75 - 1.5 * second), 3.0 / 32.0)
            scaled = [across * delta[c] for c in range(3)]
            tiles = [scaled[a] * delta[b] for a in range(3) for b in range(a, 3)]
            lefts.append(
                jnp.concatenate(
                    [along + tile if k in (0, 3, 5) else tile for k, tile in enumerate(tiles)],
                    axis=0,
                )
            )
            rights.append(block[g * WIDTH : (g + 1) * WIDTH, :])
        left = jnp.concatenate(lefts, axis=1)
        right = jnp.concatenate(rights, axis=1)
        left_high, left_low = halves(left)
        right = jnp.concatenate(halves(right), axis=0)

        def dot(part):
            return lax.dot_general(
                right, part, (((1,), (1,)), ((), ())), preferred_element_type=jnp.float32
            )

        return total + (dot(left_high) + dot(left_low))

    total = over(pairs, jnp.zeros((2 * WIDTH, 6 * targets), jnp.float32))
    total = total[:WIDTH] + total[WIDTH:]
    parts = [total[:, m * targets : (m + 1) * targets] for m in range(6)]
    tile = {}
    at = 0
    for a in range(3):
        for b in range(a, 3):
            tile[a, b] = tile[b, a] = parts[at]
            at += 1
    outs = []
    for c in range(3):
        outs.append(sum(tile[c, e][e * count : (e + 1) * count] for e in range(3)))
    rows_of = jnp.concatenate(
        centre + [jnp.where(valid, 1.0, 0.0), jnp.zeros((targets, LANES - 4), jnp.float32)], axis=1
    ).T[:8, :targets]
    there = rows_of[3:4] > 0.0
    wide = jnp.where(there, jnp.concatenate(outs + [rows_of[:3]], axis=0), 0.0)
    velocity = wide[:features]
    velocities[...] = velocity
    for c in range(3):
        lead = velocity[c * count : c * count + 1]
        rest = jnp.sum(velocity[c * count + 1 : (c + 1) * count], axis=0, keepdims=True)
        drift = step_time * lead + brown_weight * rest
        fraction[c : c + 1, :] = (wide[features + c : features + c + 1] + drift) / BOX


def body(positions, forces, owner):
    swimmers = positions.shape[1]
    features = forces.shape[0]
    wide_count = lax.axis_size("wide")
    narrow_count = lax.axis_size("narrow")
    devices = wide_count * narrow_count
    rows = swimmers * WIDTH // LANES
    vmem = pl.BlockSpec(memory_space=pltpu.VMEM)
    small = jnp.concatenate([positions.T, owner.astype(jnp.float32)], axis=1).T
    packed = pl.pallas_call(
        pack_kernel,
        out_shape=jax.ShapeDtypeStruct((devices // 2, rows, LANES), jnp.float32),
        in_specs=[vmem] * 2,
        out_specs=vmem,
        compiler_params=pltpu.CompilerParams(vmem_limit_bytes=4 << 20),
    )(small, forces.T)
    order = [
        [w * narrow_count + n for w in range(parity, wide_count, 2) for n in range(narrow_count)]
        for parity in range(2)
    ]
    own = lax.all_to_all(
        packed,
        ("wide", "narrow"),
        split_axis=0,
        concat_axis=0,
        axis_index_groups=[group[::-1] for group in order],
    )
    own = own.reshape(devices // 2 * rows, LANES)
    other = lax.ppermute(own, "wide", [(w, w ^ 1) for w in range(wide_count)])
    slots = wide_count * CAP
    return pl.pallas_call(
        functools.partial(move_kernel, rows, narrow_count, features),
        out_shape=(
            jax.ShapeDtypeStruct((3, slots), jnp.float32),
            jax.ShapeDtypeStruct((features, slots), jnp.float32),
        ),
        in_specs=[vmem] * 2,
        out_specs=(vmem, vmem),
        compiler_params=pltpu.CompilerParams(vmem_limit_bytes=16 << 20),
    )(own, other)


def solution(mesh):
    return jax.shard_map(
        body,
        mesh=mesh,
        in_specs=(
            P(None, ("wide", "narrow")),
            P(None, ("wide", "narrow")),
            P(("wide", "narrow"), None),
        ),
        out_specs=(P(None, ("wide", "narrow")), P(None, ("wide", "narrow"))),
        check_vma=False,
    )
```

```python
import functools

import jax
import jax.numpy as jnp
from jax import lax
from jax.experimental import pallas as pl
from jax.experimental.pallas import tpu as pltpu
from jax.sharding import PartitionSpec as P

BOX = 32

step_time = 0.5
brown_weight = 0.3

LANES = 128
WIDTH = 32
CAP = 2


def pack_kernel(small, forces, out):
    swimmers, features = forces.shape
    rows = swimmers * WIDTH // LANES
    square = jnp.concatenate(
        [
            jnp.zeros((features, swimmers), jnp.float32),
            small[...],
            jnp.zeros((WIDTH - features - 4, swimmers), jnp.float32),
        ],
        axis=0,
    )
    square = jnp.concatenate(
        [square, jnp.full((WIDTH, LANES - swimmers), -1.0, jnp.float32)], axis=1
    )
    row = square[features + 3 : features + 4, :]
    before = pltpu.roll(jnp.broadcast_to(row, (swimmers, LANES)), 1, 1, stride=1, stride_axis=0)
    earlier = lax.broadcasted_iota(jnp.int32, before.shape, 0) < lax.broadcasted_iota(
        jnp.int32, before.shape, 1
    )
    rank = jnp.sum(jnp.where((before == row) & earlier, 1.0, 0.0), axis=0, keepdims=True)
    at = lax.broadcasted_iota(jnp.int32, square.shape, 0)
    square = jnp.where(at == features + 4, rank, square)
    turned = jnp.concatenate(
        [square.T[:swimmers], jnp.zeros((swimmers, LANES - WIDTH), jnp.float32)], axis=1
    )
    first = jnp.concatenate(
        [forces[...], jnp.zeros((swimmers, LANES - features), jnp.float32)], axis=1
    )
    lane = lax.broadcasted_iota(jnp.int32, first.shape, 1)
    wide = jnp.where(lane < features, first, turned)
    packed = wide[:rows]
    for g in range(1, LANES // WIDTH):
        packed = packed + pltpu.roll(wide, g * WIDTH, 1)[g * rows : (g + 1) * rows]
    out[...] = jnp.broadcast_to(packed[None], out.shape)


def part_of(wide, wide_count):
    return (wide + 2 * wide // wide_count) % 2


def halves(value):
    high = value.astype(jnp.bfloat16)
    return high, (value - high.astype(jnp.float32)).astype(jnp.bfloat16)


def move_kernel(rows, narrow_count, features, own, other, fraction, velocities):
    groups = LANES // WIDTH
    count = features // 3
    targets = velocities.shape[1]
    half = LANES // 2
    chunks = own.shape[0] // half
    side = own.shape[0] // rows
    index = lax.axis_index("wide")
    mine_wide = index.astype(jnp.float32)
    mine_narrow = lax.axis_index("narrow")
    shape = (targets, LANES)
    slot = lax.broadcasted_iota(jnp.int32, shape, 0)
    giver = slot // CAP
    source = side - 1 - giver // 2 * narrow_count - mine_narrow
    wide_count = targets // CAP
    same = part_of(giver, wide_count) == part_of(index, wide_count)
    source = source + jnp.where(same, 0, side)
    wanted = (source * CAP + slot % CAP).astype(jnp.float32)
    lane = lax.broadcasted_iota(jnp.int32, (1, LANES), 1)
    device = lane // half * side + lane % half // rows
    device = (device * CAP).astype(jnp.float32)

    def turned(chunk):
        at = pl.ds(chunk * half, half)
        return jnp.concatenate([own[at, :], other[at, :]], axis=0).T

    def field(block, group, index):
        at = group * WIDTH + index
        return block[at : at + 1, :]

    def over(body, start):
        return body(0, start) if chunks == 1 else lax.fori_loop(0, chunks, body, start)

    nobody = -1e4

    def collect(chunk, carry):
        block = turned(chunk)
        here = device + jnp.float32(chunk * (half // rows) * CAP)
        for g in range(groups):
            held = here + field(block, g, features + 4)
            held = jnp.where(field(block, g, features + 3) == mine_wide, held, -1.0)
            hit = held == wanted
            carry = tuple(
                jnp.maximum(carry[c], jnp.where(hit, field(block, g, features + c), nobody))
                for c in range(3)
            )
        return carry

    centre = over(collect, (jnp.full(shape, nobody, jnp.float32),) * 3)
    centre = [jnp.max(part, axis=1, keepdims=True) for part in centre]
    valid = centre[0] > 0.5 * nobody

    def pairs(chunk, total):
        block = turned(chunk)
        lefts, rights = [], []
        for g in range(groups):
            delta = [centre[c] - field(block, g, features + c) for c in range(3)]
            square = delta[0] * delta[0] + delta[1] * delta[1] + delta[2] * delta[2]
            root = jnp.minimum(lax.rsqrt(square), 1e18)
            radius = square * root
            inverse = jnp.minimum(root, 2.0)
            far = radius >= 2.0
            second = inverse * inverse
            along = jnp.where(
                far, inverse * (0.75 + 0.5 * second), 1.0 - 9.0 / 32.0 * radius
            )
            across = inverse * jnp.where(far, second * (0.75 - 1.5 * second), 3.0 / 32.0)
            scaled = [across * delta[c] for c in range(3)]
            tiles = [scaled[a] * delta[b] for a in range(3) for b in range(a, 3)]
            lefts.append(
                jnp.concatenate(
                    [along + tile if k in (0, 3, 5) else tile for k, tile in enumerate(tiles)],
                    axis=0,
                )
            )
            rights.append(block[g * WIDTH : (g + 1) * WIDTH, :])
        left = jnp.concatenate(lefts, axis=1)
        right = jnp.concatenate(rights, axis=1)
        left_high, left_low = halves(left)
        right = jnp.concatenate(halves(right), axis=0)

        def dot(part):
            return lax.dot_general(
                right, part, (((1,), (1,)), ((), ())), preferred_element_type=jnp.float32
            )

        return total + (dot(left_high) + dot(left_low))

    total = over(pairs, jnp.zeros((2 * WIDTH, 6 * targets), jnp.float32))
    total = total[:WIDTH] + total[WIDTH:]
    parts = [total[:, m * targets : (m + 1) * targets] for m in range(6)]
    tile = {}
    at = 0
    for a in range(3):
        for b in range(a, 3):
            tile[a, b] = tile[b, a] = parts[at]
            at += 1
    outs = []
    for c in range(3):
        outs.append(sum(tile[c, e][e * count : (e + 1) * count] for e in range(3)))
    rows_of = jnp.concatenate(
        centre + [jnp.where(valid, 1.0, 0.0), jnp.zeros((targets, LANES - 4), jnp.float32)], axis=1
    ).T[:8, :targets]
    there = rows_of[3:4] > 0.0
    wide = jnp.where(there, jnp.concatenate(outs + [rows_of[:3]], axis=0), 0.0)
    velocity = wide[:features]
    velocities[...] = velocity
    for c in range(3):
        lead = velocity[c * count : c * count + 1]
        rest = jnp.sum(velocity[c * count + 1 : (c + 1) * count], axis=0, keepdims=True)
        drift = step_time * lead + brown_weight * rest
        fraction[c : c + 1, :] = (wide[features + c : features + c + 1] + drift) / BOX


def body(positions, forces, owner):
    swimmers = positions.shape[1]
    features = forces.shape[0]
    wide_count = lax.axis_size("wide")
    narrow_count = lax.axis_size("narrow")
    devices = wide_count * narrow_count
    rows = swimmers * WIDTH // LANES
    vmem = pl.BlockSpec(memory_space=pltpu.VMEM)
    small = jnp.concatenate([positions.T, owner.astype(jnp.float32)], axis=1).T
    packed = pl.pallas_call(
        pack_kernel,
        out_shape=jax.ShapeDtypeStruct((devices // 2, rows, LANES), jnp.float32),
        in_specs=[vmem] * 2,
        out_specs=vmem,
        compiler_params=pltpu.CompilerParams(vmem_limit_bytes=4 << 20),
    )(small, forces.T)
    order = [
        [
            w * narrow_count + n
            for w in range(wide_count)
            for n in range(narrow_count)
            if part_of(w, wide_count) == part
        ]
        for part in range(2)
    ]
    own = lax.all_to_all(
        packed,
        ("wide", "narrow"),
        split_axis=0,
        concat_axis=0,
        axis_index_groups=[group[::-1] for group in order],
    )
    own = own.reshape(devices // 2 * rows, LANES)
    other = lax.ppermute(own, "wide", [(w, w ^ 1) for w in range(wide_count)])
    slots = wide_count * CAP
    return pl.pallas_call(
        functools.partial(move_kernel, rows, narrow_count, features),
        out_shape=(
            jax.ShapeDtypeStruct((3, slots), jnp.float32),
            jax.ShapeDtypeStruct((features, slots), jnp.float32),
        ),
        in_specs=[vmem] * 2,
        out_specs=(vmem, vmem),
        compiler_params=pltpu.CompilerParams(vmem_limit_bytes=16 << 20),
    )(own, other)


def solution(mesh):
    return jax.shard_map(
        body,
        mesh=mesh,
        in_specs=(
            P(None, ("wide", "narrow")),
            P(None, ("wide", "narrow")),
            P(("wide", "narrow"), None),
        ),
        out_specs=(P(None, ("wide", "narrow")), P(None, ("wide", "narrow"))),
        check_vma=False,
    )
```

```python
import functools

import jax
import jax.numpy as jnp
from jax import lax
from jax.experimental import pallas as pl
from jax.experimental.pallas import tpu as pltpu
from jax.sharding import PartitionSpec as P

BOX = 32

step_time = 0.5
brown_weight = 0.3

LANES = 128
WIDTH = 32
CAP = 2


def pack_kernel(small, forces, out):
    swimmers, features = forces.shape
    rows = swimmers * WIDTH // LANES
    square = jnp.concatenate(
        [
            jnp.zeros((features, swimmers), jnp.float32),
            small[...],
            jnp.zeros((WIDTH - features - 4, swimmers), jnp.float32),
        ],
        axis=0,
    )
    square = jnp.concatenate(
        [square, jnp.full((WIDTH, LANES - swimmers), -1.0, jnp.float32)], axis=1
    )
    row = square[features + 3 : features + 4, :]
    before = pltpu.roll(jnp.broadcast_to(row, (swimmers, LANES)), 1, 1, stride=1, stride_axis=0)
    earlier = lax.broadcasted_iota(jnp.int32, before.shape, 0) < lax.broadcasted_iota(
        jnp.int32, before.shape, 1
    )
    rank = jnp.sum(jnp.where((before == row) & earlier, 1.0, 0.0), axis=0, keepdims=True)
    at = lax.broadcasted_iota(jnp.int32, square.shape, 0)
    square = jnp.where(at == features + 4, rank, square)
    turned = jnp.concatenate(
        [square.T[:swimmers], jnp.zeros((swimmers, LANES - WIDTH), jnp.float32)], axis=1
    )
    first = jnp.concatenate(
        [forces[...], jnp.zeros((swimmers, LANES - features), jnp.float32)], axis=1
    )
    lane = lax.broadcasted_iota(jnp.int32, first.shape, 1)
    wide = jnp.where(lane < features, first, turned)
    packed = wide[:rows]
    for g in range(1, LANES // WIDTH):
        packed = packed + pltpu.roll(wide, g * WIDTH, 1)[g * rows : (g + 1) * rows]
    out[...] = jnp.broadcast_to(packed[None], out.shape)


LAYER = 4


def part_of(wide):
    return (wide + wide // LAYER) % 2


def halves(value):
    high = value.astype(jnp.bfloat16)
    return high, (value - high.astype(jnp.float32)).astype(jnp.bfloat16)


def move_kernel(rows, narrow_count, features, own, other, fraction, velocities):
    groups = LANES // WIDTH
    count = features // 3
    targets = velocities.shape[1]
    half = LANES // 2
    chunks = own.shape[0] // half
    side = own.shape[0] // rows
    index = lax.axis_index("wide")
    mine_wide = index.astype(jnp.float32)
    mine_narrow = lax.axis_index("narrow")
    shape = (targets, LANES)
    slot = lax.broadcasted_iota(jnp.int32, shape, 0)
    giver = slot // CAP
    part = part_of(giver)
    source = side - 1 - giver // 2 * narrow_count - mine_narrow - part * (LAYER // 2 * narrow_count)
    source = jnp.where(source < 0, source + side, source)
    source = source + jnp.where(part == part_of(index), 0, side)
    wanted = (source * CAP + slot % CAP).astype(jnp.float32)
    lane = lax.broadcasted_iota(jnp.int32, (1, LANES), 1)
    device = lane // half * side + lane % half // rows
    device = (device * CAP).astype(jnp.float32)

    def turned(chunk):
        at = pl.ds(chunk * half, half)
        return jnp.concatenate([own[at, :], other[at, :]], axis=0).T

    def field(block, group, index):
        at = group * WIDTH + index
        return block[at : at + 1, :]

    def over(body, start):
        return body(0, start) if chunks == 1 else lax.fori_loop(0, chunks, body, start)

    nobody = -1e4

    def collect(chunk, carry):
        block = turned(chunk)
        here = device + jnp.float32(chunk * (half // rows) * CAP)
        for g in range(groups):
            held = here + field(block, g, features + 4)
            held = jnp.where(field(block, g, features + 3) == mine_wide, held, -1.0)
            hit = held == wanted
            carry = tuple(
                jnp.maximum(carry[c], jnp.where(hit, field(block, g, features + c), nobody))
                for c in range(3)
            )
        return carry

    centre = over(collect, (jnp.full(shape, nobody, jnp.float32),) * 3)
    centre = [jnp.max(part, axis=1, keepdims=True) for part in centre]
    valid = centre[0] > 0.5 * nobody

    def pairs(chunk, total):
        block = turned(chunk)
        lefts, rights = [], []
        for g in range(groups):
            delta = [centre[c] - field(block, g, features + c) for c in range(3)]
            square = delta[0] * delta[0] + delta[1] * delta[1] + delta[2] * delta[2]
            root = jnp.minimum(lax.rsqrt(square), 1e18)
            radius = square * root
            inverse = jnp.minimum(root, 2.0)
            far = radius >= 2.0
            second = inverse * inverse
            along = jnp.where(
                far, inverse * (0.75 + 0.5 * second), 1.0 - 9.0 / 32.0 * radius
            )
            across = inverse * jnp.where(far, second * (0.75 - 1.5 * second), 3.0 / 32.0)
            scaled = [across * delta[c] for c in range(3)]
            tiles = [scaled[a] * delta[b] for a in range(3) for b in range(a, 3)]
            lefts.append(
                jnp.concatenate(
                    [along + tile if k in (0, 3, 5) else tile for k, tile in enumerate(tiles)],
                    axis=0,
                )
            )
            rights.append(block[g * WIDTH : (g + 1) * WIDTH, :])
        left = jnp.concatenate(lefts, axis=1)
        right = jnp.concatenate(rights, axis=1)
        left_high, left_low = halves(left)
        right = jnp.concatenate(halves(right), axis=0)

        def dot(part):
            return lax.dot_general(
                right, part, (((1,), (1,)), ((), ())), preferred_element_type=jnp.float32
            )

        return total + (dot(left_high) + dot(left_low))

    total = over(pairs, jnp.zeros((2 * WIDTH, 6 * targets), jnp.float32))
    total = total[:WIDTH] + total[WIDTH:]
    parts = [total[:, m * targets : (m + 1) * targets] for m in range(6)]
    tile = {}
    at = 0
    for a in range(3):
        for b in range(a, 3):
            tile[a, b] = tile[b, a] = parts[at]
            at += 1
    outs = []
    for c in range(3):
        outs.append(sum(tile[c, e][e * count : (e + 1) * count] for e in range(3)))
    rows_of = jnp.concatenate(
        centre + [jnp.where(valid, 1.0, 0.0), jnp.zeros((targets, LANES - 4), jnp.float32)], axis=1
    ).T[:8, :targets]
    there = rows_of[3:4] > 0.0
    wide = jnp.where(there, jnp.concatenate(outs + [rows_of[:3]], axis=0), 0.0)
    velocity = wide[:features]
    velocities[...] = velocity
    for c in range(3):
        lead = velocity[c * count : c * count + 1]
        rest = jnp.sum(velocity[c * count + 1 : (c + 1) * count], axis=0, keepdims=True)
        drift = step_time * lead + brown_weight * rest
        fraction[c : c + 1, :] = (wide[features + c : features + c + 1] + drift) / BOX


def body(positions, forces, owner):
    swimmers = positions.shape[1]
    features = forces.shape[0]
    wide_count = lax.axis_size("wide")
    narrow_count = lax.axis_size("narrow")
    devices = wide_count * narrow_count
    rows = swimmers * WIDTH // LANES
    vmem = pl.BlockSpec(memory_space=pltpu.VMEM)
    small = jnp.concatenate([positions.T, owner.astype(jnp.float32)], axis=1).T
    packed = pl.pallas_call(
        pack_kernel,
        out_shape=jax.ShapeDtypeStruct((devices // 2, rows, LANES), jnp.float32),
        in_specs=[vmem] * 2,
        out_specs=vmem,
        compiler_params=pltpu.CompilerParams(vmem_limit_bytes=4 << 20),
    )(small, forces.T)
    order = [
        [
            w * narrow_count + n
            for w in range(wide_count)
            for n in range(narrow_count)
            if part_of(w) == part
        ]
        for part in range(2)
    ]
    layer = LAYER // 2 * narrow_count
    order = [order[0][::-1], order[1][: -layer][::-1] + order[1][-layer:][::-1]]
    own = lax.all_to_all(
        packed,
        ("wide", "narrow"),
        split_axis=0,
        concat_axis=0,
        axis_index_groups=order,
    )
    own = own.reshape(devices // 2 * rows, LANES)
    other = lax.ppermute(own, "wide", [(w, w ^ 1) for w in range(wide_count)])
    slots = wide_count * CAP
    return pl.pallas_call(
        functools.partial(move_kernel, rows, narrow_count, features),
        out_shape=(
            jax.ShapeDtypeStruct((3, slots), jnp.float32),
            jax.ShapeDtypeStruct((features, slots), jnp.float32),
        ),
        in_specs=[vmem] * 2,
        out_specs=(vmem, vmem),
        compiler_params=pltpu.CompilerParams(vmem_limit_bytes=16 << 20),
    )(own, other)


def solution(mesh):
    return jax.shard_map(
        body,
        mesh=mesh,
        in_specs=(
            P(None, ("wide", "narrow")),
            P(None, ("wide", "narrow")),
            P(("wide", "narrow"), None),
        ),
        out_specs=(P(None, ("wide", "narrow")), P(None, ("wide", "narrow"))),
        check_vma=False,
    )
```
